32 devices in a mesh: groups: 2 (over y), dp: 8 (over z, x), section: 2 (over core).
Axes of the slice: x: 2, y: 2, z: 4, core: 2. Of those that a mesh axis runs over, the one named last changes fastest.
Arguments:
- latents: bfloat16 [2048, 3072], P(('groups', 'dp')), parts along dimension 0, may hold values from -6 to 6
- out_grad: float32 [2048, 3072], P(('groups', 'dp')), parts along dimension 0, may hold values from -0.3 to 0.3
- frozen_weight: bfloat16 [2, 3072, 1536], P('section', 'dp'), may hold values from -0.109375 to 0.109375
- norm_gain: float32 [2, 3072], P('section'), may hold values from 0.5 to 1.5
- time_gate: float32 [2, 50], P('section'), may hold values from 0.5 to 2
- down_factors: bfloat16 [2, 96, 64, 3072], P('section', ('groups', 'dp')), parts along dimension 1, may hold values from -0.109375 to 0.109375
- up_factors: bfloat16 [2, 96, 64, 1536], P('section', ('groups', 'dp')), parts along dimension 1, may hold values from -0.75 to 0.75
- block_jobs: int32 [16], P('groups'), parts along dimension 0, may hold values from 0 to 47
- owners: int32 [96], P('groups'), parts along dimension 0, may hold values from 0 to 47, as said below
- block_steps: int32 [16], P(('groups', 'dp')), parts along dimension 0, may hold values from 0 to 49
- block_fill: int32 [16], P(('groups', 'dp')), parts along dimension 0, may hold values from 1 to 128, as said below
Outputs:
- grad_down: float32 [2, 96, 64, 3072], P('section', ('groups', 'dp')), parts along dimension 1
- grad_up: float32 [2, 96, 64, 1536], P('section', ('groups', 'dp')), parts along dimension 1
The draws below stay inside these ranges and needn't reach their ends.
There are 2 independent parts, one for each index of `groups`. The reference program is written for one: setup_inputs(seed, part) draws one part's arguments, and reference() takes and returns one part's arrays. A program takes and returns all parts, laid end to end along the dimension named above; an argument that names none is the same for every part. Nothing has to cross between parts.
Inputs may be any that keep to these rules, and one draw needn't show every extreme that they name: `owners`: no two adapters share a slot; slot 0 and the last slot always hold one. `block_fill`: the live rows come first in their block; in every draw some block is full and some holds a single live row.
All inputs are finite; a program needn't handle non-finite values.
Results may differ from the reference program's by a relative error of at most 0.006.
Values may be sent and summed in bfloat16 or wider, within the bound.
A program may use at most 128 MiB of HBM per device.

```python
import math
import jax
import jax.numpy as jnp
import numpy as np
from jax import lax

D = 3072
H = 1536
R = 64
ADAPTERS = 48
TSTEPS = 50
BLK = 128
SLOT_COUNT = 48
BLOCKS = 8
ROWS = 1024


def draw_owners(key, part):
    middle = jax.random.permutation(jax.random.fold_in(key, 11), SLOT_COUNT - 2).astype(jnp.int32) + 1
    picked = jnp.concatenate([jnp.zeros((1,), jnp.int32), middle[:ADAPTERS - 2], jnp.full((1,), SLOT_COUNT - 1, jnp.int32)])
    return jax.random.permutation(jax.random.fold_in(key, 12), picked).astype(jnp.int32)


def draw_block_fill(key, part):
    counts = jax.random.randint(jax.random.fold_in(key, 21), (BLOCKS,), 1, BLK + 1).astype(jnp.int32)
    full_at = jax.random.randint(jax.random.fold_in(key, 22), (), 0, BLOCKS).astype(jnp.int32)
    counts = counts.at[full_at].set(BLK)
    counts = counts.at[(full_at + 1) % BLOCKS].set(1)
    return counts.astype(jnp.int32)


def set_ends(array, rng, least, high):
    longest = array.shape.index(max(array.shape))
    spots = []
    for shift in (0, 1):
        where = [jax.random.randint(jax.random.fold_in(rng, axis), (), 0, length) for axis, length in enumerate(array.shape)]
        where[longest] = (where[longest] + shift) % array.shape[longest]
        spots.append(tuple(where))
    return array.at[spots[0]].set(least).at[spots[1]].set(high)


def level_of(stream_key, extent, cuts, smallest, high):
    gain, own = 1.0, jax.random.fold_in(stream_key, 6)
    for position, blocks in cuts:
        draws = jnp.exp(jax.random.uniform(jax.random.fold_in(own, position), (blocks,), jnp.float32, smallest / len(cuts), high / len(cuts)))
        gain = gain * jnp.repeat(draws, extent[position] // blocks).reshape([-1 if axis == position else 1 for axis in range(len(extent))])
    return gain


def cumulative_ranks(amount, lean):
    weights = [(1 << 20) // math.isqrt(standing ** lean) + 1 for standing in range(1, amount + 1)]
    spread = 1 + sum(weights) // (1 << 30)
    return np.cumsum(np.array([max(1, weight // spread) for weight in weights]))


def skewed_ids(stream_key, shape, count, skew):
    listing = cumulative_ranks(count, skew)
    ticket = jax.random.randint(jax.random.fold_in(stream_key, 1), shape, 0, int(listing[count - 1]))
    rank = jnp.searchsorted(jnp.asarray(listing, jnp.int32), ticket, side="right")
    return jax.random.permutation(jax.random.fold_in(stream_key, 2), count)[rank].astype(jnp.int32)


def scatter_about(rng, shape, spread, most, cuts=(), held_as=jnp.bfloat16):
    result = spread * jax.random.normal(rng, shape, jnp.float32)
    if cuts:
        result = result * level_of(rng, shape, cuts, -0.22, 0.18)
    return jnp.clip(result, -most, most).astype(held_as)


def setup_inputs(seed: int = 0, part: int = 0) -> dict:
    key_list = jax.random.split(jax.random.key(seed), 12)
    own_keys = jax.random.split(jax.random.fold_in(key_list[11], part), 12)
    return {
        "latents": scatter_about(own_keys[0], (ROWS, D), 1.0, 6.0, ((0, 8),)),
        "out_grad": scatter_about(own_keys[1], (ROWS, D), 0.05, 0.3, ((0, 8),), jnp.float32),
        "frozen_weight": scatter_about(key_list[2], (2, D, H), D ** -0.5, 0.109375, ((0, 2), (1, 8))),
        "norm_gain": jnp.clip(1.0 + 0.1 * jax.random.normal(key_list[3], (2, D), jnp.float32), 0.5, 1.5),
        "time_gate": jnp.clip(jnp.exp(math.log(2.0) - 1.3862944 * jax.random.uniform(key_list[4], (2, TSTEPS), jnp.float32) ** level_of(key_list[4], (2, TSTEPS), ((0, 2),), -0.2, 0.2)), 0.5, 2.0),
        "down_factors": scatter_about(own_keys[5], (2, SLOT_COUNT, R, D), D ** -0.5, 0.109375, ((0, 2), (1, 8))),
        "up_factors": scatter_about(own_keys[6], (2, SLOT_COUNT, R, H), R ** -0.5, 0.75, ((0, 2), (1, 8))),
        "block_jobs": set_ends(skewed_ids(own_keys[7], (BLOCKS,), ADAPTERS, 2), jax.random.fold_in(own_keys[7], 3), 0, ADAPTERS - 1).astype(jnp.int32),
        "owners": draw_owners(jax.random.fold_in(jax.random.fold_in(key_list[11], part), 71), part),
        "block_steps": set_ends(jax.random.randint(own_keys[9], (BLOCKS,), 0, TSTEPS), jax.random.fold_in(own_keys[9], 1), 0, TSTEPS - 1).astype(jnp.int32),
        "block_fill": draw_block_fill(jax.random.fold_in(jax.random.fold_in(key_list[11], part), 71), part),
    }


epsilon = 1e-06

def matrix_product(spec, left_op, right_op):
    return jnp.einsum(spec, left_op.astype(jnp.float32), right_op.astype(jnp.float32), precision=lax.Precision.HIGHEST)

def forward_pass(inputs, frozen_layer, gain_row, down_projection_block, up_block, scales):
    out_width = up_block.shape[2]
    values = inputs.astype(jnp.float32)
    inverse = lax.rsqrt(lax.optimization_barrier(jnp.mean(values * values, axis=2)) + epsilon)
    normalized_input = (values * inverse[:, :, None] * gain_row).astype(jnp.bfloat16)
    frozen_out = matrix_product('bmd,dh->bmh', normalized_input, frozen_layer)
    reduced_features = matrix_product('uyi,uoi->uyo', normalized_input, down_projection_block).astype(jnp.bfloat16)
    extra = matrix_product('bmq,bqh->bmh', reduced_features, up_block)
    update = scales[:, None, None] * (frozen_out + extra)
    window_out = (values[:, :, :out_width] + update).astype(jnp.bfloat16)
    outputs = jnp.concatenate([window_out, inputs[:, :, out_width:]], axis=2)
    return (outputs, normalized_input, inverse, reduced_features)

def backward_pass(inputs, normalized_input, inverse, reduced_features, cotangent, frozen_layer, gain_row, down_projection_block, up_block, scales):
    out_width = up_block.shape[2]
    values = inputs.astype(jnp.float32)
    delta_output = (scales[:, None, None] * cotangent[:, :, :out_width]).astype(jnp.bfloat16)
    grad_upper = matrix_product('bmq,bmh->bqh', reduced_features, delta_output)
    low_rank_delta = matrix_product('bmh,bqh->bmq', delta_output, up_block).astype(jnp.bfloat16)
    lower_gradient = matrix_product('hoc,hou->hcu', low_rank_delta, normalized_input)
    delta_normalized = matrix_product('way,cy->wac', delta_output, frozen_layer) + matrix_product('rha,rak->rhk', low_rank_delta, down_projection_block)
    scaled = gain_row * delta_normalized
    inner = lax.optimization_barrier(jnp.mean(values * scaled, axis=2))
    cubed = inverse * inverse * inverse
    delta_in = inverse[:, :, None] * scaled - values * (cubed * inner)[:, :, None]
    carried = (cotangent + delta_in).astype(jnp.bfloat16)
    return (carried, lower_gradient, grad_upper)

def reference(latents, out_grad, frozen_weight, norm_gain, time_gate, down_factors, up_factors, block_jobs, owners, block_steps, block_fill):
    slot_of = owners[block_jobs].astype(jnp.int32)
    inputs = latents.reshape(BLOCKS, BLK, D)
    live_rows = jnp.arange(BLK, dtype=jnp.int32)[None, :] < block_fill[:, None]
    cotangent = jnp.where(live_rows[:, :, None], out_grad.reshape(BLOCKS, BLK, D), 0.0)
    stored = []
    for layer_index in range(2):
        down_projection_block = down_factors[layer_index][slot_of]
        up_block = up_factors[layer_index][slot_of]
        scales = time_gate[layer_index][block_steps]
        outputs, normalized_input, inverse, reduced_features = forward_pass(inputs, frozen_weight[layer_index], norm_gain[layer_index], down_projection_block, up_block, scales)
        stored.append((inputs, normalized_input, inverse, reduced_features, down_projection_block, up_block, scales))
        inputs = outputs
    results = []
    for layer_index in (1, 0):
        saved_in, normalized_input, inverse, reduced_features, down_projection_block, up_block, scales = stored[layer_index]
        carried, lower_gradient, grad_upper = backward_pass(saved_in, normalized_input, inverse, reduced_features, cotangent, frozen_weight[layer_index], norm_gain[layer_index], down_projection_block, up_block, scales)
        cotangent = carried.astype(jnp.float32)
        summed_down = jax.ops.segment_sum(lower_gradient, slot_of, num_segments=SLOT_COUNT)
        summed_up = jax.ops.segment_sum(grad_upper, slot_of, num_segments=SLOT_COUNT)
        results.append((summed_down, summed_up))
    grad_down = jnp.stack([results[1][0], results[0][0]])
    grad_up = jnp.stack([results[1][1], results[0][1]])
    return (grad_down, grad_up)
```

```python
import jax
import jax.numpy as jnp
from jax import lax
from jax.sharding import PartitionSpec as P

epsilon = 1e-06
f32 = jnp.float32
bf16 = jnp.bfloat16


def dot(left, right, dims):
    return lax.dot_general(left, right, (dims, ((), ())), preferred_element_type=f32)


def body(
    latents,
    out_grad,
    frozen_weight,
    norm_gain,
    time_gate,
    down_factors,
    up_factors,
    block_jobs,
    owners,
    block_steps,
    block_fill,
):
    is_first = lax.axis_index("section") == 0
    place = lax.axis_index("dp")
    slot_local, low_rank, width = down_factors.shape[1:]
    out_width = up_factors.shape[3]
    blocks_dev = block_fill.shape[0]
    rows = latents.shape[0] // blocks_dev
    gain = norm_gain[0]
    gate = time_gate[0]

    frozen = lax.all_gather(frozen_weight[0], "dp", axis=0, tiled=True)

    matches = block_jobs[:, None] == jnp.arange(owners.shape[0], dtype=jnp.int32)[None, :]
    slot_of = jnp.sum(jnp.where(matches, owners[None, :], 0), axis=1)
    first_slot = place * slot_local
    mine = [(slot_of == first_slot + j)[:, None, None] for j in range(slot_local)]

    def spread(factors):
        total = jnp.zeros((), bf16)
        for j in range(slot_local):
            total = jnp.where(mine[j], factors[j][None], total)
        return total

    down = lax.psum_scatter(spread(down_factors[0]), "dp", scatter_dimension=0, tiled=True)
    up = lax.psum_scatter(spread(up_factors[0]), "dp", scatter_dimension=0, tiled=True)

    chosen = block_steps[:, None] == jnp.arange(gate.shape[0], dtype=jnp.int32)[None, :]
    scales = jnp.sum(jnp.where(chosen, gate[None, :], 0.0), axis=1)
    row_scale = jnp.repeat(scales, rows)[:, None]
    live = (jnp.arange(rows, dtype=jnp.int32)[None, :] < block_fill[:, None]).reshape(-1, 1)
    masked = jnp.where(live, out_grad, 0.0)

    def per_block(left, right, dims):
        left = left.reshape(blocks_dev, -1, left.shape[-1])
        return [dot(left[b], right[b], dims) for b in range(blocks_dev)]

    def forward(x):
        values = x.astype(f32)
        inverse = lax.rsqrt(jnp.mean(values * values, axis=1, keepdims=True) + epsilon)
        normed = (values * inverse * gain[None, :]).astype(bf16)
        low = jnp.concatenate(per_block(normed, down, ((1,), (1,)))).astype(bf16)
        return values, inverse, normed, low

    def layer_out(x, values, normed, low):
        extra = jnp.concatenate(per_block(low, up, ((1,), (0,))))
        update = row_scale * (dot(normed, frozen, ((1,), (0,))) + extra)
        return (values[:, :out_width] + update).astype(bf16)

    pair = [(0, 1)]
    values, inverse, normed, low = forward(latents)
    window = layer_out(latents, values, normed, low)
    window = lax.ppermute(window, "section", pair)
    x = jnp.where(is_first, latents, jnp.concatenate([window, latents[:, out_width:]], axis=1))
    values, inverse, normed, low = forward(x)

    head = masked[:, :out_width]
    delta = (row_scale * head).astype(bf16)
    low_grad = jnp.concatenate(per_block(delta, up, ((1,), (1,)))).astype(bf16)
    norm_grad = dot(delta, frozen, ((1,), (1,))) + jnp.concatenate(
        per_block(low_grad, down, ((1,), (0,)))
    )
    scaled = gain[None, :] * norm_grad
    inner = jnp.mean(values * scaled, axis=1, keepdims=True)
    cubed = inverse * inverse * inverse
    carried = (
        head
        + inverse * scaled[:, :out_width]
        - values[:, :out_width] * (cubed * inner)
    ).astype(bf16)
    carried = lax.ppermute(carried, "section", [(1, 0)])
    head = jnp.where(is_first, carried.astype(f32), head)
    delta = (row_scale * head).astype(bf16)
    low_grad = jnp.concatenate(per_block(delta, up, ((1,), (1,)))).astype(bf16)

    def outer(left, right):
        left = left.reshape(blocks_dev, rows, -1)
        right = right.reshape(blocks_dev, rows, -1)
        return jnp.stack([dot(left[b], right[b], ((0,), (0,))) for b in range(blocks_dev)])

    grad_down = outer(low_grad, normed).astype(bf16)
    grad_up = outer(low, delta).astype(bf16)
    all_down = lax.all_gather(grad_down, "dp", axis=0, tiled=True)
    all_up = lax.all_gather(grad_up, "dp", axis=0, tiled=True)

    def gather_slots(grads):
        slots = []
        for j in range(slot_local):
            slots.append(jnp.sum(jnp.where(mine[j], grads.astype(f32), 0.0), axis=0))
        return jnp.stack(slots)[None]

    return gather_slots(all_down), gather_slots(all_up)


def solution(mesh):
    placed = (
        P(("groups", "dp"), None),
        P(("groups", "dp"), None),
        P("section", "dp", None),
        P("section", None),
        P("section", None),
        P("section", ("groups", "dp"), None, None),
        P("section", ("groups", "dp"), None, None),
        P("groups"),
        P("groups"),
        P(("groups", "dp")),
        P(("groups", "dp")),
    )
    return jax.shard_map(
        body,
        mesh=mesh,
        in_specs=placed,
        out_specs=(
            P("section", ("groups", "dp"), None, None),
            P("section", ("groups", "dp"), None, None),
        ),
        check_vma=False,
    )
```

```python
import functools

import jax
import jax.numpy as jnp
from jax import lax
from jax.experimental import pallas as pl
from jax.experimental.pallas import tpu as pltpu
from jax.sharding import PartitionSpec as P

epsilon = 1e-06
f32 = jnp.float32
bf16 = jnp.bfloat16


def dot(left, right, dims):
    return lax.dot_general(left, right, (dims, ((), ())), preferred_element_type=f32)


MESH = pl.DeviceIdType.MESH


def ring_index(spot, n):
    spot = lax.rem(spot + 2 * n, n)
    half = (n + 1) // 2
    return jnp.where(spot < half, 2 * spot, 2 * (n - 1 - spot) + 1)


def ring_spot(index, n):
    return jnp.where(lax.rem(index, 2) == 0, index // 2, n - 1 - index // 2)


def remote(src, dst, send, recv, **where):
    return pltpu.make_async_remote_copy(
        src_ref=src,
        dst_ref=dst,
        send_sem=send,
        recv_sem=recv,
        device_id=where,
        device_id_type=MESH,
    )


def greet(*places):
    barrier = pltpu.get_barrier_semaphore()
    for where in places:
        pl.semaphore_signal(barrier, inc=1, device_id=where, device_id_type=MESH)
    pl.semaphore_wait(barrier, len(places))


def fetch_kernel(
    n, w_ref, f_ref, w_out, f_out, acc, own, w_send, w_recv, y_send, y_recv, f_send, f_recv, local
):
    depth = w_ref.shape[0]
    quarter = depth // 4
    half = f_ref.shape[1] // 2
    plane = lax.axis_index("groups")
    p = ring_spot(lax.axis_index("dp"), n)
    nexts = (ring_index(p + 1, n), ring_index(p - 1, n))
    greet({"dp": nexts[0]}, {"dp": nexts[1]}, {"groups": 1 - plane})

    def piece(owner, part):
        start = pl.multiple_of(owner * depth + part * quarter, quarter)
        return w_out.at[pl.ds(start, quarter)]

    def w_copy(way, step):
        part = 2 * plane + way
        owner = ring_index(p - step if way == 0 else p + step, n)
        target = piece(owner, part)
        start = pl.multiple_of(part * quarter, quarter)
        source = w_ref.at[pl.ds(start, quarter)] if step == 0 else target
        return remote(
            source, target, w_send.at[way, step], w_recv.at[way, step], dp=nexts[way]
        )

    def w_arrival(way, step):
        owner = ring_index(p - 1 - step if way == 0 else p + 1 + step, n)
        target = piece(owner, 2 * plane + way)
        return remote(
            target, target, w_send.at[way, step], w_recv.at[way, step], dp=nexts[way]
        )

    def y_copy(way, step, part):
        owner = ring_index(p - 1 - step if way == 0 else p + 1 + step, n)
        target = piece(owner, part)
        return remote(
            target, target, y_send.at[way, step], y_recv.at[way, step], groups=1 - plane
        )

    def f_rows(way):
        return pl.ds(way * half, half)

    def f_copy(way, step):
        block = ring_index(p - 1 - step if way == 0 else p + 1 + step, n)
        source = own.at[block, f_rows(way)] if step == 0 else acc.at[way, step - 1]
        return remote(
            source, acc.at[way, step], f_send.at[way, step], f_recv.at[way, step], dp=nexts[way]
        )

    for way in range(2):
        w_copy(way, 0).start()
    mine = pltpu.make_async_copy(f_ref, own, local.at[0])
    mine.start()
    start = pl.multiple_of(lax.axis_index("dp") * depth, depth)
    keep = pltpu.make_async_copy(w_ref, w_out.at[pl.ds(start, depth)], local.at[1])
    keep.start()
    mine.wait()
    for way in range(2):
        f_copy(way, 0).start()

    last = n - 2
    for step in range(n - 1):
        for way in range(2):
            w_arrival(way, step).wait_recv()
            if step < last:
                w_copy(way, step + 1).start()
            y_copy(way, step, 2 * plane + way).start()
        for way in range(2):
            f_copy(way, step).wait_recv()
            block = ring_index(p - 2 - step if way == 0 else p + 2 + step, n)
            total = acc[way, step] + own[block, f_rows(way)]
            if step < last:
                acc[way, step] = total
                f_copy(way, step + 1).start()
            else:
                f_out[f_rows(way)] = total
    for step in range(n - 1):
        for way in range(2):
            y_copy(way, step, 2 * (1 - plane) + way).wait_recv()
            w_copy(way, step).wait_send()
            f_copy(way, step).wait_send()
            y_copy(way, step, 2 * plane + way).wait_send()
    keep.wait()


def fetch(n, w, f):
    depth, columns = w.shape
    blocks, rank, cut = f.shape
    steps = (2, n - 1)
    pairs = [pltpu.SemaphoreType.DMA(steps)] * 6
    return pl.pallas_call(
        functools.partial(fetch_kernel, n),
        out_shape=(
            jax.ShapeDtypeStruct((n * depth, columns), w.dtype),
            jax.ShapeDtypeStruct((rank, cut), f.dtype),
        ),
        in_specs=[pl.BlockSpec(memory_space=pl.ANY)] * 2,
        out_specs=(
            pl.BlockSpec(memory_space=pl.ANY),
            pl.BlockSpec(memory_space=pltpu.VMEM),
        ),
        scratch_shapes=[
            pltpu.VMEM((2, n - 1, rank // 2, cut), f.dtype),
            pltpu.VMEM((blocks, rank, cut), f.dtype),
            *pairs,
            pltpu.SemaphoreType.DMA((2,)),
        ],
        compiler_params=pltpu.CompilerParams(
            collective_id=0, has_side_effects=True, vmem_limit_bytes=32 << 20
        ),
        name="fetch",
    )(w, f)


def share_kernel(n, g_ref, g_out, send, recv, local):
    half = g_ref.shape[0] // 2
    me = lax.axis_index("dp")
    p = ring_spot(me, n)
    nexts = (ring_index(p + 1, n), ring_index(p - 1, n))
    greet({"dp": nexts[0]}, {"dp": nexts[1]})

    def copy(way, step):
        owner = ring_index(p - step if way == 0 else p + step, n)
        part = pl.ds(way * half, half)
        target = g_out.at[owner, part]
        source = g_ref.at[part] if step == 0 else target
        return remote(source, target, send.at[way, step], recv.at[way, step], dp=nexts[way])

    def arrival(way, step):
        owner = ring_index(p - 1 - step if way == 0 else p + 1 + step, n)
        target = g_out.at[owner, pl.ds(way * half, half)]
        return remote(target, target, send.at[way, step], recv.at[way, step], dp=nexts[way])

    for way in range(2):
        copy(way, 0).start()
    keep = pltpu.make_async_copy(g_ref, g_out.at[me], local.at[0])
    keep.start()
    for step in range(n - 1):
        for way in range(2):
            arrival(way, step).wait_recv()
            if step < n - 2:
                copy(way, step + 1).start()
    for step in range(n - 1):
        for way in range(2):
            copy(way, step).wait_send()
    keep.wait()


def share(n, g):
    rank, cut = g.shape
    pairs = [pltpu.SemaphoreType.DMA((2, n - 1))] * 2
    return pl.pallas_call(
        functools.partial(share_kernel, n),
        out_shape=jax.ShapeDtypeStruct((n, rank, cut), g.dtype),
        in_specs=[pl.BlockSpec(memory_space=pl.ANY)],
        out_specs=pl.BlockSpec(memory_space=pl.ANY),
        scratch_shapes=[*pairs, pltpu.SemaphoreType.DMA((1,))],
        compiler_params=pltpu.CompilerParams(collective_id=1, has_side_effects=True),
        name="share",
    )(g)


def body(
    latents,
    out_grad,
    frozen_weight,
    norm_gain,
    time_gate,
    down_factors,
    up_factors,
    block_jobs,
    owners,
    block_steps,
    block_fill,
):
    is_first = lax.axis_index("section") == 0
    place = lax.axis_index("dp")
    slot_local, low_rank, width = down_factors.shape[1:]
    out_width = up_factors.shape[3]
    blocks_dev = block_fill.shape[0]
    rows = latents.shape[0] // blocks_dev
    gain = norm_gain[0]
    gate = time_gate[0]

    lanes = lax.axis_size("dp")
    ringed = (
        3 <= lanes <= 16
        and lax.axis_size("groups") == 2
        and blocks_dev == 1
        and frozen_weight.shape[1] % 64 == 0
        and low_rank % 32 == 0
    )

    matches = block_jobs[:, None] == jnp.arange(owners.shape[0], dtype=jnp.int32)[None, :]
    slot_of = jnp.sum(jnp.where(matches, owners[None, :], 0), axis=1)
    first_slot = place * slot_local
    mine = [(slot_of == first_slot + j)[:, None, None] for j in range(slot_local)]

    def spread(factors):
        total = jnp.zeros((), bf16)
        for j in range(slot_local):
            total = jnp.where(mine[j], factors[j][None], total)
        return total

    if ringed:
        sent = jnp.concatenate([spread(down_factors[0]), spread(up_factors[0])], axis=2)
        frozen, factors = fetch(lanes, frozen_weight[0], sent)
        down = factors[None, :, :width]
        up = factors[None, :, width:]
    else:
        frozen = lax.all_gather(frozen_weight[0], "dp", axis=0, tiled=True)
        down = lax.psum_scatter(spread(down_factors[0]), "dp", scatter_dimension=0, tiled=True)
        up = lax.psum_scatter(spread(up_factors[0]), "dp", scatter_dimension=0, tiled=True)

    chosen = block_steps[:, None] == jnp.arange(gate.shape[0], dtype=jnp.int32)[None, :]
    scales = jnp.sum(jnp.where(chosen, gate[None, :], 0.0), axis=1)
    row_scale = jnp.repeat(scales, rows)[:, None]
    live = (jnp.arange(rows, dtype=jnp.int32)[None, :] < block_fill[:, None]).reshape(-1, 1)
    masked = jnp.where(live, out_grad, 0.0)

    def per_block(left, right, dims):
        left = left.reshape(blocks_dev, -1, left.shape[-1])
        return [dot(left[b], right[b], dims) for b in range(blocks_dev)]

    def forward(x):
        values = x.astype(f32)
        inverse = lax.rsqrt(jnp.mean(values * values, axis=1, keepdims=True) + epsilon)
        normed = (values * inverse * gain[None, :]).astype(bf16)
        low = jnp.concatenate(per_block(normed, down, ((1,), (1,)))).astype(bf16)
        return values, inverse, normed, low

    def layer_out(x, values, normed, low):
        extra = jnp.concatenate(per_block(low, up, ((1,), (0,))))
        update = row_scale * (dot(normed, frozen, ((1,), (0,))) + extra)
        return (values[:, :out_width] + update).astype(bf16)

    pair = [(0, 1)]
    values, inverse, normed, low = forward(latents)
    window = layer_out(latents, values, normed, low)
    window = lax.ppermute(window, "section", pair)
    x = jnp.where(is_first, latents, jnp.concatenate([window, latents[:, out_width:]], axis=1))
    values, inverse, normed, low = forward(x)

    head = masked[:, :out_width]
    delta = (row_scale * head).astype(bf16)
    low_grad = jnp.concatenate(per_block(delta, up, ((1,), (1,)))).astype(bf16)
    norm_grad = dot(delta, frozen, ((1,), (1,))) + jnp.concatenate(
        per_block(low_grad, down, ((1,), (0,)))
    )
    scaled = gain[None, :] * norm_grad
    inner = jnp.mean(values * scaled, axis=1, keepdims=True)
    cubed = inverse * inverse * inverse
    carried = (
        head
        + inverse * scaled[:, :out_width]
        - values[:, :out_width] * (cubed * inner)
    ).astype(bf16)
    carried = lax.ppermute(carried, "section", [(1, 0)])
    head = jnp.where(is_first, carried.astype(f32), head)
    delta = (row_scale * head).astype(bf16)
    low_grad = jnp.concatenate(per_block(delta, up, ((1,), (1,)))).astype(bf16)

    def outer(left, right):
        left = left.reshape(blocks_dev, rows, -1)
        right = right.reshape(blocks_dev, rows, -1)
        return jnp.stack([dot(left[b], right[b], ((0,), (0,))) for b in range(blocks_dev)])

    grad_down = outer(low_grad, normed).astype(bf16)
    grad_up = outer(low, delta).astype(bf16)
    if ringed:
        shared = share(lanes, jnp.concatenate([grad_down[0], grad_up[0]], axis=1))
        all_down, all_up = shared[:, :, :width], shared[:, :, width:]
    else:
        all_down = lax.all_gather(grad_down, "dp", axis=0, tiled=True)
        all_up = lax.all_gather(grad_up, "dp", axis=0, tiled=True)

    def gather_slots(grads):
        slots = []
        for j in range(slot_local):
            slots.append(jnp.sum(jnp.where(mine[j], grads.astype(f32), 0.0), axis=0))
        return jnp.stack(slots)[None]

    return gather_slots(all_down), gather_slots(all_up)


def solution(mesh):
    placed = (
        P(("groups", "dp"), None),
        P(("groups", "dp"), None),
        P("section", "dp", None),
        P("section", None),
        P("section", None),
        P("section", ("groups", "dp"), None, None),
        P("section", ("groups", "dp"), None, None),
        P("groups"),
        P("groups"),
        P(("groups", "dp")),
        P(("groups", "dp")),
    )
    return jax.shard_map(
        body,
        mesh=mesh,
        in_specs=placed,
        out_specs=(
            P("section", ("groups", "dp"), None, None),
            P("section", ("groups", "dp"), None, None),
        ),
        check_vma=False,
    )
```

```python
import functools

import jax
import jax.numpy as jnp
from jax import lax
from jax.experimental import pallas as pl
from jax.experimental.pallas import tpu as pltpu
from jax.sharding import PartitionSpec as P

epsilon = 1e-06
f32 = jnp.float32
bf16 = jnp.bfloat16


def dot(left, right, dims):
    return lax.dot_general(left, right, (dims, ((), ())), preferred_element_type=f32)


MESH = pl.DeviceIdType.MESH


def ring_index(spot, n):
    spot = lax.rem(spot + 2 * n, n)
    half = (n + 1) // 2
    return jnp.where(spot < half, 2 * spot, 2 * (n - 1 - spot) + 1)


def ring_spot(index, n):
    return jnp.where(lax.rem(index, 2) == 0, index // 2, n - 1 - index // 2)


def remote(src, dst, send, recv, **where):
    return pltpu.make_async_remote_copy(
        src_ref=src,
        dst_ref=dst,
        send_sem=send,
        recv_sem=recv,
        device_id=where,
        device_id_type=MESH,
    )


def greet(*places):
    barrier = pltpu.get_barrier_semaphore()
    for where in places:
        pl.semaphore_signal(barrier, inc=1, device_id=where, device_id_type=MESH)
    pl.semaphore_wait(barrier, len(places))


def fetch_kernel(
    n, w_ref, f_ref, w_out, f_out, acc, own, w_send, w_recv, y_send, y_recv, f_send, f_recv, local
):
    depth = w_ref.shape[0]
    quarter = depth // 4
    half = f_ref.shape[1] // 2
    plane = lax.axis_index("groups")
    p = ring_spot(lax.axis_index("dp"), n)
    nexts = (ring_index(p + 1, n), ring_index(p - 1, n))
    greet({"dp": nexts[0]}, {"dp": nexts[1]}, {"groups": 1 - plane})

    def piece(owner, part):
        start = pl.multiple_of(owner * depth + part * quarter, quarter)
        return w_out.at[pl.ds(start, quarter)]

    def w_copy(way, step):
        part = 2 * plane + way
        owner = ring_index(p - step if way == 0 else p + step, n)
        target = piece(owner, part)
        start = pl.multiple_of(part * quarter, quarter)
        source = w_ref.at[pl.ds(start, quarter)] if step == 0 else target
        return remote(
            source, target, w_send.at[way, step], w_recv.at[way, step], dp=nexts[way]
        )

    def w_arrival(way, step):
        owner = ring_index(p - 1 - step if way == 0 else p + 1 + step, n)
        target = piece(owner, 2 * plane + way)
        return remote(
            target, target, w_send.at[way, step], w_recv.at[way, step], dp=nexts[way]
        )

    def y_copy(way, step, part):
        owner = ring_index(p - 1 - step if way == 0 else p + 1 + step, n)
        target = piece(owner, part)
        return remote(
            target, target, y_send.at[way, step], y_recv.at[way, step], groups=1 - plane
        )

    def f_rows(way):
        return pl.ds(way * half, half)

    def f_copy(way, step):
        block = ring_index(p - 1 - step if way == 0 else p + 1 + step, n)
        source = own.at[block, f_rows(way)] if step == 0 else acc.at[way, step - 1]
        return remote(
            source, acc.at[way, step], f_send.at[way, step], f_recv.at[way, step], dp=nexts[way]
        )

    for way in range(2):
        w_copy(way, 0).start()
    mine = pltpu.make_async_copy(f_ref, own, local.at[0])
    mine.start()
    start = pl.multiple_of(lax.axis_index("dp") * depth, depth)
    keep = pltpu.make_async_copy(w_ref, w_out.at[pl.ds(start, depth)], local.at[1])
    keep.start()
    mine.wait()
    for way in range(2):
        f_copy(way, 0).start()

    last = n - 2
    for step in range(n - 1):
        for way in range(2):
            w_arrival(way, step).wait_recv()
            if step < last:
                w_copy(way, step + 1).start()
            y_copy(way, step, 2 * plane + way).start()
        for way in range(2):
            f_copy(way, step).wait_recv()
            block = ring_index(p - 2 - step if way == 0 else p + 2 + step, n)
            total = acc[way, step] + own[block, f_rows(way)]
            if step < last:
                acc[way, step] = total
                f_copy(way, step + 1).start()
            else:
                f_out[f_rows(way)] = total
    for step in range(n - 1):
        for way in range(2):
            y_copy(way, step, 2 * (1 - plane) + way).wait_recv()
            w_copy(way, step).wait_send()
            f_copy(way, step).wait_send()
            y_copy(way, step, 2 * plane + way).wait_send()
    keep.wait()


def fetch(n, w, f):
    depth, columns = w.shape
    blocks, rank, cut = f.shape
    steps = (2, n - 1)
    pairs = [pltpu.SemaphoreType.DMA(steps)] * 6
    return pl.pallas_call(
        functools.partial(fetch_kernel, n),
        out_shape=(
            jax.ShapeDtypeStruct((n * depth, columns), w.dtype),
            jax.ShapeDtypeStruct((rank, cut), f.dtype),
        ),
        in_specs=[pl.BlockSpec(memory_space=pl.ANY)] * 2,
        out_specs=(
            pl.BlockSpec(memory_space=pl.ANY),
            pl.BlockSpec(memory_space=pltpu.VMEM),
        ),
        scratch_shapes=[
            pltpu.VMEM((2, n - 1, rank // 2, cut), f.dtype),
            pltpu.VMEM((blocks, rank, cut), f.dtype),
            *pairs,
            pltpu.SemaphoreType.DMA((2,)),
        ],
        compiler_params=pltpu.CompilerParams(
            collective_id=0, has_side_effects=True, vmem_limit_bytes=32 << 20
        ),
        name="fetch",
    )(w, f)


def share_kernel(n, cuts, g_ref, g_out, send, recv, local):
    piece = g_ref.shape[0] // (2 * cuts)
    me = lax.axis_index("dp")
    p = ring_spot(me, n)
    nexts = (ring_index(p + 1, n), ring_index(p - 1, n))
    greet({"dp": nexts[0]}, {"dp": nexts[1]})

    def rows(way, cut):
        return pl.ds((way * cuts + cut) * piece, piece)

    def copy(way, step, cut):
        owner = ring_index(p - step if way == 0 else p + step, n)
        part = rows(way, cut)
        target = g_out.at[owner, part]
        source = g_ref.at[part] if step == 0 else target
        return remote(
            source, target, send.at[way, step, cut], recv.at[way, step, cut], dp=nexts[way]
        )

    def arrival(way, step, cut):
        owner = ring_index(p - 1 - step if way == 0 else p + 1 + step, n)
        target = g_out.at[owner, rows(way, cut)]
        return remote(
            target, target, send.at[way, step, cut], recv.at[way, step, cut], dp=nexts[way]
        )

    for cut in range(cuts):
        for way in range(2):
            copy(way, 0, cut).start()
    keep = pltpu.make_async_copy(g_ref, g_out.at[me], local.at[0])
    keep.start()
    for step in range(n - 1):
        for cut in range(cuts):
            for way in range(2):
                arrival(way, step, cut).wait_recv()
                if step < n - 2:
                    copy(way, step + 1, cut).start()
    for step in range(n - 1):
        for cut in range(cuts):
            for way in range(2):
                copy(way, step, cut).wait_send()
    keep.wait()


def share(n, g):
    rank, cut = g.shape
    cuts = 2
    pairs = [pltpu.SemaphoreType.DMA((2, n - 1, cuts))] * 2
    return pl.pallas_call(
        functools.partial(share_kernel, n, cuts),
        out_shape=jax.ShapeDtypeStruct((n, rank, cut), g.dtype),
        in_specs=[pl.BlockSpec(memory_space=pl.ANY)],
        out_specs=pl.BlockSpec(memory_space=pl.ANY),
        scratch_shapes=[*pairs, pltpu.SemaphoreType.DMA((1,))],
        compiler_params=pltpu.CompilerParams(collective_id=1, has_side_effects=True),
        name="share",
    )(g)


def settle_kernel(slot_ref, first_ref, g_ref, down_ref, up_ref):
    width = down_ref.shape[3]
    slot = first_ref[0] + pl.program_id(0)
    down_ref[...] = jnp.zeros_like(down_ref)
    up_ref[...] = jnp.zeros_like(up_ref)
    for block in range(g_ref.shape[0]):

        @pl.when(slot_ref[block] == slot)
        def _():
            down_ref[0, 0] += g_ref[block, :, :width].astype(f32)
            up_ref[0, 0] += g_ref[block, :, width:].astype(f32)


def settle(slot_of, first_slot, shared, slot_local, width):
    blocks, rank, cut = shared.shape

    def out_block(columns):
        return pl.BlockSpec((1, 1, rank, columns), lambda j, *_: (0, j, 0, 0))

    return pl.pallas_call(
        settle_kernel,
        grid_spec=pltpu.PrefetchScalarGridSpec(
            num_scalar_prefetch=2,
            grid=(slot_local,),
            in_specs=[pl.BlockSpec((blocks, rank, cut), lambda j, *_: (0, 0, 0))],
            out_specs=[out_block(width), out_block(cut - width)],
        ),
        out_shape=[
            jax.ShapeDtypeStruct((1, slot_local, rank, width), f32),
            jax.ShapeDtypeStruct((1, slot_local, rank, cut - width), f32),
        ],
        compiler_params=pltpu.CompilerParams(vmem_limit_bytes=32 << 20),
        name="settle",
    )(slot_of, jnp.reshape(first_slot, (1,)), shared)


def body(
    latents,
    out_grad,
    frozen_weight,
    norm_gain,
    time_gate,
    down_factors,
    up_factors,
    block_jobs,
    owners,
    block_steps,
    block_fill,
):
    is_first = lax.axis_index("section") == 0
    place = lax.axis_index("dp")
    slot_local, low_rank, width = down_factors.shape[1:]
    out_width = up_factors.shape[3]
    blocks_dev = block_fill.shape[0]
    rows = latents.shape[0] // blocks_dev
    gain = norm_gain[0]
    gate = time_gate[0]

    lanes = lax.axis_size("dp")
    ringed = (
        3 <= lanes <= 16
        and lax.axis_size("groups") == 2
        and blocks_dev == 1
        and frozen_weight.shape[1] % 64 == 0
        and low_rank % 32 == 0
    )

    matches = block_jobs[:, None] == jnp.arange(owners.shape[0], dtype=jnp.int32)[None, :]
    slot_of = jnp.sum(jnp.where(matches, owners[None, :], 0), axis=1)
    first_slot = place * slot_local
    mine = [(slot_of == first_slot + j)[:, None, None] for j in range(slot_local)]

    def spread(factors):
        total = jnp.zeros((), bf16)
        for j in range(slot_local):
            total = jnp.where(mine[j], factors[j][None], total)
        return total

    chosen = block_steps[:, None] == jnp.arange(gate.shape[0], dtype=jnp.int32)[None, :]
    scales = jnp.sum(jnp.where(chosen, gate[None, :], 0.0), axis=1)
    row_scale = jnp.repeat(scales, rows)[:, None]
    live = (jnp.arange(rows, dtype=jnp.int32)[None, :] < block_fill[:, None]).reshape(-1, 1)

    head = jnp.where(live, out_grad[:, :out_width], 0.0)
    delta = (row_scale * head).astype(bf16)
    start_values = latents.astype(f32)
    start_inverse = lax.rsqrt(jnp.mean(start_values * start_values, axis=1, keepdims=True) + epsilon)
    start_normed = (start_values * start_inverse * gain[None, :]).astype(bf16)
    start_normed, delta = lax.optimization_barrier((start_normed, delta))

    if ringed:
        sent = jnp.concatenate([spread(down_factors[0]), spread(up_factors[0])], axis=2)
        frozen, factors = fetch(lanes, frozen_weight[0], sent)
        down = factors[None, :, :width]
        up = factors[None, :, width:]
    else:
        frozen = lax.all_gather(frozen_weight[0], "dp", axis=0, tiled=True)
        down = lax.psum_scatter(spread(down_factors[0]), "dp", scatter_dimension=0, tiled=True)
        up = lax.psum_scatter(spread(up_factors[0]), "dp", scatter_dimension=0, tiled=True)

    def per_block(left, right, dims):
        left = left.reshape(blocks_dev, -1, left.shape[-1])
        return [dot(left[b], right[b], dims) for b in range(blocks_dev)]

    def forward(x):
        values = x.astype(f32)
        inverse = lax.rsqrt(jnp.mean(values * values, axis=1, keepdims=True) + epsilon)
        normed = (values * inverse * gain[None, :]).astype(bf16)
        low = jnp.concatenate(per_block(normed, down, ((1,), (1,)))).astype(bf16)
        return values, inverse, normed, low

    def layer_out(x, values, normed, low):
        extra = jnp.concatenate(per_block(low, up, ((1,), (0,))))
        update = row_scale * (dot(normed, frozen, ((1,), (0,))) + extra)
        return (values[:, :out_width] + update).astype(bf16)

    pair = [(0, 1)]
    low = jnp.concatenate(per_block(start_normed, down, ((1,), (1,)))).astype(bf16)
    window = layer_out(latents, start_values, start_normed, low)
    window = lax.ppermute(window, "section", pair)
    x = jnp.where(is_first, latents, jnp.concatenate([window, latents[:, out_width:]], axis=1))
    values, inverse, normed, low = forward(x)

    low_grad = jnp.concatenate(per_block(delta, up, ((1,), (1,)))).astype(bf16)
    norm_grad = dot(delta, frozen, ((1,), (1,))) + jnp.concatenate(
        per_block(low_grad, down, ((1,), (0,)))
    )
    scaled = gain[None, :] * norm_grad
    inner = jnp.mean(values * scaled, axis=1, keepdims=True)
    cubed = inverse * inverse * inverse
    carried = (
        head
        + inverse * scaled[:, :out_width]
        - values[:, :out_width] * (cubed * inner)
    ).astype(bf16)
    carried = lax.ppermute(carried, "section", [(1, 0)])
    head = jnp.where(is_first, carried.astype(f32), head)
    delta = (row_scale * head).astype(bf16)
    low_grad = jnp.concatenate(per_block(delta, up, ((1,), (1,)))).astype(bf16)

    def outer(left, right):
        left = left.reshape(blocks_dev, rows, -1)
        right = right.reshape(blocks_dev, rows, -1)
        return jnp.stack([dot(left[b], right[b], ((0,), (0,))) for b in range(blocks_dev)])

    grad_down = outer(low_grad, normed).astype(bf16)
    grad_up = outer(low, delta).astype(bf16)
    if ringed:
        shared = share(lanes, jnp.concatenate([grad_down[0], grad_up[0]], axis=1))
        return settle(slot_of, first_slot, shared, slot_local, width)
    else:
        all_down = lax.all_gather(grad_down, "dp", axis=0, tiled=True)
        all_up = lax.all_gather(grad_up, "dp", axis=0, tiled=True)

    def gather_slots(grads):
        slots = []
        for j in range(slot_local):
            slots.append(jnp.sum(jnp.where(mine[j], grads.astype(f32), 0.0), axis=0))
        return jnp.stack(slots)[None]

    return gather_slots(all_down), gather_slots(all_up)


def solution(mesh):
    placed = (
        P(("groups", "dp"), None),
        P(("groups", "dp"), None),
        P("section", "dp", None),
        P("section", None),
        P("section", None),
        P("section", ("groups", "dp"), None, None),
        P("section", ("groups", "dp"), None, None),
        P("groups"),
        P("groups"),
        P(("groups", "dp")),
        P(("groups", "dp")),
    )
    return jax.shard_map(
        body,
        mesh=mesh,
        in_specs=placed,
        out_specs=(
            P("section", ("groups", "dp"), None, None),
            P("section", ("groups", "dp"), None, None),
        ),
        check_vma=False,
    )
```
